32 devices in a mesh: row: 16 (over z, x, core), col: 2 (over y).
Axes of the slice: x: 2, y: 2, z: 4, core: 2. Of those that a mesh axis runs over, the one named last changes fastest.
Arguments:
- amplitudes: bfloat16 [64, 640000], P(('row', 'col')), may hold values from -6 to 6
- integrals: bfloat16 [2, 800, 640000], P(None, None, ('row', 'col')), may hold values from -0.0078125 to 0.0078125
Outputs:
- ladder: float32 [64, 2, 800], P(('row', 'col'))
The draws below stay inside these ranges and needn't reach their ends.
All inputs are finite; a program needn't handle non-finite values.
Results may differ from the reference program's by a relative error of at most 0.0003.
Values may be sent and summed in bfloat16 or wider, within the bound.
No kernel may reach another device: no remote copies, remote signals or barrier semaphores. Data moves between devices by JAX's collectives and lax.ppermute only.
A program may use at most 128 MiB of HBM per device.

```python
import jax
import jax.numpy as jnp
from jax import lax

NV = 800
A_WIN = 2
PAIRS = 64


def levels(rng, shape, cuts, smallest, top_value):
    level, own = 1.0, jax.random.fold_in(rng, 6)
    for position, parts in cuts:
        heights = jnp.exp(jax.random.uniform(jax.random.fold_in(own, position), (parts,), jnp.float32, smallest / len(cuts), top_value / len(cuts)))
        level = level * jnp.repeat(heights, shape[position] // parts).reshape([-1 if axis == position else 1 for axis in range(len(shape))])
    return level


def normal_values(key, shape, scale, most, shards=(), kind=jnp.bfloat16):
    drawn = jax.random.normal(key, shape, jnp.float32) * scale
    if len(shards) > 0:
        drawn = levels(key, shape, shards, -0.22, 0.18) * drawn
    return jnp.clip(drawn, min=-most, max=most).astype(kind)


def setup_inputs(seed: int = 0) -> dict:
    streams_of = jax.random.split(jax.random.key(seed), 3)
    amplitudes = normal_values(streams_of[0], (PAIRS, NV * NV), 1.0, 6.0, ((0, 32),))
    integrals = normal_values(streams_of[1], (A_WIN, NV, NV * NV), (NV * NV) ** -0.5, 0.0078125, ((2, 32),))
    return {"amplitudes": amplitudes, "integrals": integrals}


def reference(amplitudes, integrals):
    ladder_slabs = []
    for window_index in range(A_WIN):
        ladder_slabs.append(lax.dot_general(amplitudes, integrals[window_index], (((1,), (1,)), ((), ())), preferred_element_type=jnp.float32))
    return jnp.stack(ladder_slabs, axis=1)
```

```python
import jax
import jax.numpy as jnp
from jax import lax
from jax.sharding import PartitionSpec as P

BOTH = ("row", "col")


def shards(amplitudes, integrals):
    count = lax.axis_size("row") * lax.axis_size("col")
    pair_local, full_width = amplitudes.shape
    slab = full_width // count
    window, virtuals, _ = integrals.shape
    sectioned = amplitudes.reshape(pair_local, count, slab).transpose(1, 0, 2)
    local_amps = lax.all_to_all(sectioned, BOTH, split_axis=0, concat_axis=0, tiled=True)
    local_amps = local_amps.reshape(count * pair_local, slab)
    product = lax.dot_general(
        local_amps,
        integrals.reshape(window * virtuals, slab),
        (((1,), (1,)), ((), ())),
        preferred_element_type=jnp.float32,
    )
    partial = product.reshape(count, pair_local, window * virtuals)
    parts = lax.all_to_all(partial, BOTH, split_axis=0, concat_axis=0, tiled=True)
    return parts.sum(axis=0).reshape(pair_local, window, virtuals)


def solution(mesh):
    return jax.shard_map(
        shards,
        mesh=mesh,
        in_specs=(P(BOTH, None), P(None, None, BOTH)),
        out_specs=P(BOTH, None, None),
        check_vma=False,
    )
```

```python
import jax
import jax.numpy as jnp
from jax import lax
from jax.sharding import Mesh, PartitionSpec as P

ALL = ("outer", "core", "col")
CHUNKS = 4


def shards(amplitudes, integrals):
    outer, core, col = (lax.axis_size(name) for name in ALL)
    count = outer * core * col
    pair_local, full_width = amplitudes.shape
    slab = full_width // count
    window, virtuals, _ = integrals.shape
    flat = integrals.reshape(window * virtuals, slab)
    sectioned = amplitudes.reshape(pair_local, count, slab).transpose(1, 0, 2)
    step = -(-slab // CHUNKS // 128) * 128
    product = 0
    for lo in range(0, slab, step):
        hi = min(slab, lo + step)
        part = lax.all_to_all(sectioned[:, :, lo:hi], ALL, split_axis=0, concat_axis=0, tiled=True)
        product += lax.dot_general(
            part.reshape(count * pair_local, hi - lo),
            flat[:, lo:hi],
            (((1,), (1,)), ((), ())),
            preferred_element_type=jnp.float32,
        )
    partial = product.reshape(outer, core, col * pair_local, window * virtuals)
    me = lax.axis_index("core")
    own = lax.dynamic_index_in_dim(partial, me, 1, keepdims=False)
    other = lax.dynamic_index_in_dim(partial, 1 - me, 1, keepdims=False)
    own = own + lax.ppermute(other, "core", [(0, 1), (1, 0)])
    own = own.reshape(outer * col, pair_local, window * virtuals)
    parts = lax.all_to_all(own, ("outer", "col"), split_axis=0, concat_axis=0, tiled=True)
    return parts.sum(axis=0).reshape(pair_local, window, virtuals)


def solution(mesh):
    devices = mesh.devices
    split = Mesh(devices.reshape(devices.shape[0] // 2, 2, devices.shape[1]), ALL)
    return jax.shard_map(
        shards,
        mesh=split,
        in_specs=(P(ALL, None), P(None, None, ALL)),
        out_specs=P(ALL, None, None),
        check_vma=False,
    )
```

```python
import functools

import jax
import jax.numpy as jnp
from jax import lax
from jax.experimental import pallas as pl
from jax.experimental.pallas import tpu as pltpu
from jax.sharding import Mesh, PartitionSpec as P

ALL = ("z", "x", "core", "col")
LANES = 128
BLOCK = 1024
FIRST = 0.7


def window_kernel(starts, width, x_ref, o_ref, sems):
    total = x_ref.shape[1]
    copies = []
    for index, start in enumerate(starts):
        size = min(width, total - start)
        copies.append(
            pltpu.make_async_copy(
                x_ref.at[:, pl.ds(start, size)],
                o_ref.at[index, :, pl.ds(0, size)],
                sems.at[index],
            )
        )
    for copy in copies:
        copy.start()
    for copy in copies:
        copy.wait()


def windows(x, starts, width):
    return pl.pallas_call(
        functools.partial(window_kernel, starts, width),
        out_shape=jax.ShapeDtypeStruct((len(starts), x.shape[0], width), x.dtype),
        in_specs=[pl.BlockSpec(memory_space=pl.ANY)],
        out_specs=pl.BlockSpec(memory_space=pl.ANY),
        scratch_shapes=[pltpu.SemaphoreType.DMA((len(starts),))],
        cost_estimate=pl.CostEstimate(
            flops=0, bytes_accessed=4 * len(starts) * x.shape[0] * width, transcendentals=0
        ),
        name="windows",
    )(x)


def product_kernel(steps, tail_width, has_sum, off_ref, amps_ref, ints_ref, *rest):
    sum_ref = rest[0] if has_sum else None
    out_ref, acc_ref = rest[-2:]
    step = pl.program_id(0)
    off = off_ref[0]
    back = off_ref[1]
    pairs = amps_ref.shape[0]
    lane = lax.broadcasted_iota(jnp.int32, (pairs, LANES), 1)
    from_here = lane < LANES - off

    @pl.when(step == 0)
    def _():
        acc_ref[...] = jnp.zeros_like(acc_ref)

    def tiles(base, count, limit):
        rolled = []
        for t in range(min(count + 1, limit)):
            tile = amps_ref[:, pl.ds(pl.multiple_of(base + t * LANES, LANES), LANES)]
            rolled.append(pltpu.roll(tile.astype(jnp.float32), back, 1))
        return [
            jnp.where(from_here, rolled[t], rolled[min(t + 1, len(rolled) - 1)])
            for t in range(count)
        ]

    def dot(ints, amps):
        return lax.dot_general(
            ints, amps, (((1,), (1,)), ((), ())), preferred_element_type=jnp.float32
        )

    def full():
        parts = tiles(step * BLOCK, BLOCK // LANES, BLOCK // LANES + 1)
        amps = jnp.concatenate([p.astype(jnp.bfloat16) for p in parts], axis=1)
        acc_ref[...] += dot(ints_ref[...], amps)

    def tail():
        count = -(-tail_width // LANES)
        base = (steps - 1) * BLOCK
        parts = tiles(base, count, (amps_ref.shape[1] - base) // LANES)
        whole = tail_width // LANES
        if whole:
            amps = jnp.concatenate([p.astype(jnp.bfloat16) for p in parts[:whole]], axis=1)
            acc_ref[...] += dot(ints_ref[:, : whole * LANES], amps)
        if whole < count:
            valid = tail_width - whole * LANES
            amps = jnp.where(lane < valid, parts[whole], 0.0).astype(jnp.bfloat16)
            ints = ints_ref[:, whole * LANES : count * LANES]
            place = lax.broadcasted_iota(jnp.int32, ints.shape, 1)
            ints = jnp.where(place < valid, ints, jnp.zeros_like(ints))
            acc_ref[...] += dot(ints, amps)

    if tail_width == BLOCK:
        full()
    else:
        if steps > 1:
            pl.when(step < steps - 1)(full)
        pl.when(step == steps - 1)(tail)

    @pl.when(step == steps - 1)
    def _():
        result = acc_ref[...].T
        out_ref[...] = result + sum_ref[...] if has_sum else result


def product(shift, amps, flat, low, high, total):
    pairs = amps.shape[0]
    rows = flat.shape[0]
    width = high - low
    steps = -(-width // BLOCK)
    first = low // BLOCK
    whole = pl.BlockSpec((pairs, rows), lambda j: (0, 0))
    sums = [] if total is None else [total]
    return pl.pallas_call(
        functools.partial(product_kernel, steps, width - (steps - 1) * BLOCK, bool(sums)),
        out_shape=jax.ShapeDtypeStruct((pairs, rows), jnp.float32),
        grid=(steps,),
        in_specs=[
            pl.BlockSpec(memory_space=pltpu.SMEM),
            pl.BlockSpec(amps.shape, lambda j: (0, 0)),
            pl.BlockSpec((rows, BLOCK), lambda j: (0, first + j)),
        ]
        + [whole] * len(sums),
        out_specs=whole,
        scratch_shapes=[pltpu.VMEM((rows, pairs), jnp.float32)],
        compiler_params=pltpu.CompilerParams(vmem_limit_bytes=32 * 1024 * 1024),
        cost_estimate=pl.CostEstimate(
            flops=2 * pairs * rows * width, bytes_accessed=2 * rows * width, transcendentals=0
        ),
        name="product",
    )(shift, amps, flat, *sums)


def exchange_sum(blocks, names):
    count = blocks.shape[0]
    me = lax.axis_index(names)
    terms = [lax.dynamic_index_in_dim(blocks, me, 0, keepdims=False)]
    power = count & (count - 1) == 0
    for step in range(count - 1, 0, -1):
        to = (lambda i: i ^ step) if power else (lambda i: (i + step) % count)
        block = lax.dynamic_index_in_dim(blocks, to(me), 0, keepdims=False)
        terms.append(lax.ppermute(block, names, [(i, to(i)) for i in range(count)]))
    return sum(terms[1:], terms[0])


def shards(amplitudes, integrals):
    z, x, core, col = (lax.axis_size(name) for name in ALL)
    count = z * x * core * col
    pair_local, full_width = amplitudes.shape
    slab = full_width // count
    window, virtuals, _ = integrals.shape
    rows = window * virtuals
    flat = integrals.reshape(rows, slab)

    begins = [d * slab // LANES * LANES for d in range(count)]
    most = max(1, max(d * slab - begins[d] for d in range(count)))
    off = lax.rem(lax.axis_index(ALL) * slab, LANES)
    shift = jnp.stack([off, lax.rem(LANES - off, LANES)]).astype(jnp.int32)

    blocks = -(-slab // BLOCK)
    cut = max(1, min(blocks - 1, round(FIRST * blocks))) * BLOCK
    total = None
    for low, high in ((0, cut), (cut, slab)):
        width = -(-(most + high - low) // LANES) * LANES
        sent = windows(amplitudes, [b + low for b in begins], width)
        got = lax.all_to_all(sent, ALL, split_axis=0, concat_axis=0, tiled=True)
        got = got.reshape(count * pair_local, width)
        total = product(shift, got, flat, low, high, total)

    part = total.reshape(z, x, core, col, pair_local, rows)
    part = exchange_sum(part.transpose(2, 0, 1, 3, 4, 5).reshape(core, z, x * col, pair_local, rows), "core")
    part = exchange_sum(part.transpose(1, 0, 2, 3), ("x", "col"))
    part = exchange_sum(part, "z")
    return part.reshape(pair_local, window, virtuals)


def solution(mesh):
    devices = mesh.devices
    row, col = devices.shape
    split = Mesh(devices.reshape(row // 4, 2, 2, col), ALL)
    return jax.shard_map(
        shards,
        mesh=split,
        in_specs=(P(ALL, None), P(None, None, ALL)),
        out_specs=P(ALL, None, None),
        check_vma=False,
    )
```

```python
import functools

import jax
import jax.numpy as jnp
from jax import lax
from jax.experimental import pallas as pl
from jax.experimental.pallas import tpu as pltpu
from jax.sharding import Mesh, PartitionSpec as P

ALL = ("z", "x", "core", "col")
LANES = 128
BLOCK = 2560
FIRST = 0.7


def window_kernel(starts, x_ref, o_ref):
    width = o_ref.shape[2]
    for index, start in enumerate(starts):
        size = min(width, x_ref.shape[1] - start)
        o_ref[index, :, pl.ds(0, size)] = x_ref[:, pl.ds(start, size)]


def windows(x, starts, width):
    return pl.pallas_call(
        functools.partial(window_kernel, starts),
        out_shape=jax.ShapeDtypeStruct((len(starts), x.shape[0], width), x.dtype),
        in_specs=[pl.BlockSpec(memory_space=pltpu.VMEM)],
        out_specs=pl.BlockSpec(memory_space=pltpu.VMEM),
        compiler_params=pltpu.CompilerParams(vmem_limit_bytes=16 * 1024 * 1024),
        cost_estimate=pl.CostEstimate(
            flops=0, bytes_accessed=4 * len(starts) * x.shape[0] * width, transcendentals=0
        ),
        name="windows",
    )(x)


def product_kernel(steps, tail_width, has_sum, off_ref, amps_ref, ints_ref, *rest):
    sum_ref = rest[0] if has_sum else None
    out_ref, acc_ref = rest[-2:]
    step = pl.program_id(0)
    off = off_ref[0]
    back = off_ref[1]
    pairs = amps_ref.shape[0]
    lane = lax.broadcasted_iota(jnp.int32, (pairs, LANES), 1)
    from_here = lane < LANES - off

    @pl.when(step == 0)
    def _():
        acc_ref[...] = jnp.zeros_like(acc_ref)

    def tiles(base, count, limit):
        rolled = []
        for t in range(min(count + 1, limit)):
            tile = amps_ref[:, pl.ds(pl.multiple_of(base + t * LANES, LANES), LANES)]
            rolled.append(pltpu.roll(tile.astype(jnp.float32), back, 1))
        return [
            jnp.where(from_here, rolled[t], rolled[min(t + 1, len(rolled) - 1)])
            for t in range(count)
        ]

    def dot(ints, amps):
        return lax.dot_general(
            ints, amps, (((1,), (1,)), ((), ())), preferred_element_type=jnp.float32
        )

    def full():
        parts = tiles(step * BLOCK, BLOCK // LANES, BLOCK // LANES + 1)
        amps = jnp.concatenate([p.astype(jnp.bfloat16) for p in parts], axis=1)
        acc_ref[...] += dot(ints_ref[...], amps)

    def tail():
        count = -(-tail_width // LANES)
        base = (steps - 1) * BLOCK
        parts = tiles(base, count, (amps_ref.shape[1] - base) // LANES)
        whole = tail_width // LANES
        if whole:
            amps = jnp.concatenate([p.astype(jnp.bfloat16) for p in parts[:whole]], axis=1)
            acc_ref[...] += dot(ints_ref[:, : whole * LANES], amps)
        if whole < count:
            valid = tail_width - whole * LANES
            amps = jnp.where(lane < valid, parts[whole], 0.0).astype(jnp.bfloat16)
            ints = ints_ref[:, whole * LANES : count * LANES]
            place = lax.broadcasted_iota(jnp.int32, ints.shape, 1)
            ints = jnp.where(place < valid, ints, jnp.zeros_like(ints))
            acc_ref[...] += dot(ints, amps)

    if tail_width == BLOCK:
        full()
    else:
        if steps > 1:
            pl.when(step < steps - 1)(full)
        pl.when(step == steps - 1)(tail)

    @pl.when(step == steps - 1)
    def _():
        result = acc_ref[...].T
        out_ref[...] = result + sum_ref[...] if has_sum else result


def product(shift, amps, flat, low, high, total):
    pairs = amps.shape[0]
    rows = flat.shape[0]
    width = high - low
    steps = -(-width // BLOCK)
    first = low // BLOCK
    whole = pl.BlockSpec((pairs, rows), lambda j: (0, 0))
    sums = [] if total is None else [total]
    return pl.pallas_call(
        functools.partial(product_kernel, steps, width - (steps - 1) * BLOCK, bool(sums)),
        out_shape=jax.ShapeDtypeStruct((pairs, rows), jnp.float32),
        grid=(steps,),
        in_specs=[
            pl.BlockSpec(memory_space=pltpu.SMEM),
            pl.BlockSpec(amps.shape, lambda j: (0, 0)),
            pl.BlockSpec((rows, BLOCK), lambda j: (0, first + j)),
        ]
        + [whole] * len(sums),
        out_specs=whole,
        scratch_shapes=[pltpu.VMEM((rows, pairs), jnp.float32)],
        compiler_params=pltpu.CompilerParams(vmem_limit_bytes=36 * 1024 * 1024),
        cost_estimate=pl.CostEstimate(
            flops=2 * pairs * rows * width, bytes_accessed=2 * rows * width, transcendentals=0
        ),
        name="product",
    )(shift, amps, flat, *sums)


def exchange_sum(blocks, name):
    count = blocks.shape[0]
    me = lax.axis_index(name)
    if count & (count - 1):
        return lax.psum_scatter(blocks, name, scatter_dimension=0, tiled=False)
    while blocks.shape[0] > 1:
        half = blocks.shape[0] // 2
        halves = blocks.reshape(2, half, *blocks.shape[1:])
        mine = (me // half) % 2
        there = lax.dynamic_index_in_dim(halves, 1 - mine, 0, keepdims=False)
        here = lax.dynamic_index_in_dim(halves, mine, 0, keepdims=False)
        blocks = here + lax.ppermute(there, name, [(i, i ^ half) for i in range(count)])
    return blocks[0]


def shards(amplitudes, integrals):
    z, x, core, col = (lax.axis_size(name) for name in ALL)
    count = z * x * core * col
    pair_local, full_width = amplitudes.shape
    slab = full_width // count
    window, virtuals, _ = integrals.shape
    rows = window * virtuals
    flat = integrals.reshape(rows, slab)

    begins = [d * slab // LANES * LANES for d in range(count)]
    most = max(1, max(d * slab - begins[d] for d in range(count)))
    off = lax.rem(lax.axis_index(ALL) * slab, LANES)
    shift = jnp.stack([off, lax.rem(LANES - off, LANES)]).astype(jnp.int32)

    blocks = -(-slab // BLOCK)
    cut = max(1, min(blocks - 1, round(FIRST * blocks))) * BLOCK
    parts = [(0, cut), (cut, slab)] if cut < slab else [(0, slab)]
    widths = [-(-(most + high - low) // LANES) * LANES for low, high in parts]
    sent = [windows(amplitudes, [b + low for b in begins], w) for (low, _), w in zip(parts, widths)]
    got = []
    for block in sent:
        if got:
            block, got[-1] = lax.optimization_barrier((block, got[-1]))
        got.append(lax.all_to_all(block, ALL, split_axis=0, concat_axis=0, tiled=True))
    total = None
    for (low, high), width, block in zip(parts, widths, got):
        amps = block.reshape(count * pair_local, width)
        total = product(shift, amps, flat, low, high, total)

    part = total.reshape(z, x, core, col, pair_local, rows)
    part = exchange_sum(part.transpose(2, 1, 3, 0, 4, 5), "core")
    part = exchange_sum(part, "x")
    part = exchange_sum(part, "col")
    part = exchange_sum(part, "z")
    return part.reshape(pair_local, window, virtuals)


def solution(mesh):
    devices = mesh.devices
    row, col = devices.shape
    split = Mesh(devices.reshape(row // 4, 2, 2, col), ALL)
    return jax.shard_map(
        shards,
        mesh=split,
        in_specs=(P(ALL, None), P(None, None, ALL)),
        out_specs=P(ALL, None, None),
        check_vma=False,
    )
```

```python
import functools

import jax
import jax.numpy as jnp
from jax import lax
from jax.experimental import pallas as pl
from jax.experimental.pallas import tpu as pltpu
from jax.sharding import Mesh, PartitionSpec as P

ALL = ("z", "x", "core", "col")
LANES = 128
BLOCK = 1280
BUFFERS = 4
FIRST = 0.75


def window_kernel(starts, x_ref, o_ref):
    width = o_ref.shape[2]
    for index, start in enumerate(starts):
        size = min(width, x_ref.shape[1] - start)
        o_ref[index, :, pl.ds(0, size)] = x_ref[:, pl.ds(start, size)]


def windows(x, starts, width):
    return pl.pallas_call(
        functools.partial(window_kernel, starts),
        out_shape=jax.ShapeDtypeStruct((len(starts), x.shape[0], width), x.dtype),
        in_specs=[pl.BlockSpec(memory_space=pltpu.VMEM)],
        out_specs=pl.BlockSpec(memory_space=pltpu.VMEM),
        compiler_params=pltpu.CompilerParams(vmem_limit_bytes=16 * 1024 * 1024),
        cost_estimate=pl.CostEstimate(
            flops=0, bytes_accessed=4 * len(starts) * x.shape[0] * width, transcendentals=0
        ),
        name="windows",
    )(x)


def product_kernel(first, steps, tail_width, has_sum, off_ref, amps_ref, ints_hbm, *rest):
    sum_ref = rest[0] if has_sum else None
    out_ref, acc_ref = rest[-2:]
    off = off_ref[0]
    back = off_ref[1]
    pairs = amps_ref.shape[0]
    lane = lax.broadcasted_iota(jnp.int32, (pairs, LANES), 1)
    from_here = lane < LANES - off
    acc_ref[...] = jnp.zeros_like(acc_ref)

    def tiles(base, count, limit):
        rolled = []
        for t in range(min(count + 1, limit)):
            tile = amps_ref[:, pl.ds(pl.multiple_of(base + t * LANES, LANES), LANES)]
            rolled.append(pltpu.roll(tile.astype(jnp.float32), back, 1))
        return [
            jnp.where(from_here, rolled[t], rolled[min(t + 1, len(rolled) - 1)])
            for t in range(count)
        ]

    def dot(ints, amps):
        return lax.dot_general(
            ints, amps, (((1,), (1,)), ((), ())), preferred_element_type=jnp.float32
        )

    def body(ints_ref):
        step = pl.program_id(0)

        def full():
            parts = tiles(step * BLOCK, BLOCK // LANES, BLOCK // LANES + 1)
            amps = jnp.concatenate([p.astype(jnp.bfloat16) for p in parts], axis=1)
            acc_ref[...] += dot(ints_ref[...], amps)

        def tail():
            count = -(-tail_width // LANES)
            base = (steps - 1) * BLOCK
            parts = tiles(base, count, (amps_ref.shape[1] - base) // LANES)
            whole = tail_width // LANES
            if whole:
                amps = jnp.concatenate([p.astype(jnp.bfloat16) for p in parts[:whole]], axis=1)
                acc_ref[...] += dot(ints_ref[:, : whole * LANES], amps)
            if whole < count:
                valid = tail_width - whole * LANES
                amps = jnp.where(lane < valid, parts[whole], 0.0).astype(jnp.bfloat16)
                ints = ints_ref[:, whole * LANES : count * LANES]
                place = lax.broadcasted_iota(jnp.int32, ints.shape, 1)
                ints = jnp.where(place < valid, ints, jnp.zeros_like(ints))
                acc_ref[...] += dot(ints, amps)

        if tail_width == BLOCK:
            full()
        else:
            if steps > 1:
                pl.when(step < steps - 1)(full)
            pl.when(step == steps - 1)(tail)

    spec = pl.BlockSpec(
        (ints_hbm.shape[0], BLOCK),
        lambda j: (0, first + j),
        pipeline_mode=pl.Buffered(BUFFERS),
    )
    pltpu.emit_pipeline(body, grid=(steps,), in_specs=[spec])(ints_hbm)
    result = acc_ref[...].T
    out_ref[...] = result + sum_ref[...] if has_sum else result


def product(shift, amps, flat, low, high, total):
    pairs = amps.shape[0]
    rows = flat.shape[0]
    width = high - low
    steps = -(-width // BLOCK)
    whole = pl.BlockSpec(memory_space=pltpu.VMEM)
    sums = [] if total is None else [total]
    tail_width = width - (steps - 1) * BLOCK
    return pl.pallas_call(
        functools.partial(product_kernel, low // BLOCK, steps, tail_width, bool(sums)),
        out_shape=jax.ShapeDtypeStruct((pairs, rows), jnp.float32),
        in_specs=[
            pl.BlockSpec(memory_space=pltpu.SMEM),
            whole,
            pl.BlockSpec(memory_space=pl.ANY),
        ]
        + [whole] * len(sums),
        out_specs=whole,
        scratch_shapes=[pltpu.VMEM((rows, pairs), jnp.float32)],
        compiler_params=pltpu.CompilerParams(vmem_limit_bytes=24 * 1024 * 1024),
        cost_estimate=pl.CostEstimate(
            flops=2 * pairs * rows * width, bytes_accessed=2 * rows * width, transcendentals=0
        ),
        name="product",
    )(shift, amps, flat, *sums)


def exchange_sum(blocks, names):
    count = blocks.shape[0]
    me = lax.axis_index(names)
    terms = [lax.dynamic_index_in_dim(blocks, me, 0, keepdims=False)]
    power = count & (count - 1) == 0
    for step in range(count - 1, 0, -1):
        to = (lambda i: i ^ step) if power else (lambda i: (i + step) % count)
        block = lax.dynamic_index_in_dim(blocks, to(me), 0, keepdims=False)
        terms.append(lax.ppermute(block, names, [(i, to(i)) for i in range(count)]))
    return sum(terms[1:], terms[0])


def shards(amplitudes, integrals):
    z, x, core, col = (lax.axis_size(name) for name in ALL)
    count = z * x * core * col
    pair_local, full_width = amplitudes.shape
    slab = full_width // count
    window, virtuals, _ = integrals.shape
    rows = window * virtuals
    flat = integrals.reshape(rows, slab)

    begins = [d * slab // LANES * LANES for d in range(count)]
    most = max(1, max(d * slab - begins[d] for d in range(count)))
    off = lax.rem(lax.axis_index(ALL) * slab, LANES)
    shift = jnp.stack([off, lax.rem(LANES - off, LANES)]).astype(jnp.int32)

    blocks = -(-slab // BLOCK)
    cut = max(1, min(blocks - 1, round(FIRST * blocks))) * BLOCK
    parts = [(0, cut), (cut, slab)] if cut < slab else [(0, slab)]
    widths = [-(-(most + high - low) // LANES) * LANES for low, high in parts]
    sent = [windows(amplitudes, [b + low for b in begins], w) for (low, _), w in zip(parts, widths)]
    got = []
    for block in sent:
        if got:
            block, got[-1] = lax.optimization_barrier((block, got[-1]))
        got.append(lax.all_to_all(block, ALL, split_axis=0, concat_axis=0, tiled=True))
    total = None
    for (low, high), width, block in zip(parts, widths, got):
        amps = block.reshape(count * pair_local, width)
        total = product(shift, amps, flat, low, high, total)

    part = total.reshape(z, x, core, col, pair_local, rows)
    part = exchange_sum(part.transpose(2, 0, 1, 3, 4, 5).reshape(core, z, x * col, pair_local, rows), "core")
    part = exchange_sum(part.transpose(1, 0, 2, 3), ("x", "col"))
    part = exchange_sum(part, "z")
    return part.reshape(pair_local, window, virtuals)


def solution(mesh):
    devices = mesh.devices
    row, col = devices.shape
    split = Mesh(devices.reshape(row // 4, 2, 2, col), ALL)
    return jax.shard_map(
        shards,
        mesh=split,
        in_specs=(P(ALL, None), P(None, None, ALL)),
        out_specs=P(ALL, None, None),
        check_vma=False,
    )
```

```python
import functools

import jax
import jax.numpy as jnp
from jax import lax
from jax.experimental import pallas as pl
from jax.experimental.pallas import tpu as pltpu
from jax.sharding import Mesh, PartitionSpec as P

ALL = ("z", "x", "core", "col")
LANES = 128
BLOCK = 1280
BUFFERS = 3
LIMIT = 20 * 1024 * 1024
FIRST = 0.7


def window_kernel(starts, x_ref, o_ref):
    width = o_ref.shape[2]
    for index, start in enumerate(starts):
        size = min(width, x_ref.shape[1] - start)
        o_ref[index, :, pl.ds(0, size)] = x_ref[:, pl.ds(start, size)]


def windows(x, starts, width):
    return pl.pallas_call(
        functools.partial(window_kernel, starts),
        out_shape=jax.ShapeDtypeStruct((len(starts), x.shape[0], width), x.dtype),
        in_specs=[pl.BlockSpec(memory_space=pltpu.VMEM)],
        out_specs=pl.BlockSpec(memory_space=pltpu.VMEM),
        compiler_params=pltpu.CompilerParams(vmem_limit_bytes=16 * 1024 * 1024),
        cost_estimate=pl.CostEstimate(
            flops=0, bytes_accessed=4 * len(starts) * x.shape[0] * width, transcendentals=0
        ),
        name="windows",
    )(x)


def dot(ints, amps):
    return lax.dot_general(ints, amps, (((1,), (1,)), ((), ())), preferred_element_type=jnp.float32)


def shifted(off_ref, amps_ref, base, count, limit):
    lane = lax.broadcasted_iota(jnp.int32, (amps_ref.shape[0], LANES), 1)
    from_here = lane < LANES - off_ref[0]
    rolled = []
    for t in range(min(count + 1, limit)):
        tile = amps_ref[:, pl.ds(pl.multiple_of(base + t * LANES, LANES), LANES)]
        rolled.append(pltpu.roll(tile.astype(jnp.float32), off_ref[1], 1))
    return [
        jnp.where(from_here, rolled[t], rolled[min(t + 1, len(rolled) - 1)]) for t in range(count)
    ]


def first_kernel(steps, off_ref, amps_ref, ints_hbm, out_ref, acc_ref):
    acc_ref[...] = jnp.zeros_like(acc_ref)

    def body(ints_ref):
        step = pl.program_id(0)
        parts = shifted(off_ref, amps_ref, step * BLOCK, BLOCK // LANES, BLOCK // LANES + 1)
        amps = jnp.concatenate([p.astype(jnp.bfloat16) for p in parts], axis=1)
        acc_ref[...] += dot(ints_ref[...], amps)

    spec = pl.BlockSpec(
        (ints_hbm.shape[0], BLOCK), lambda j: (0, j), pipeline_mode=pl.Buffered(BUFFERS)
    )
    pltpu.emit_pipeline(body, grid=(steps,), in_specs=[spec])(ints_hbm)
    out_ref[...] = acc_ref[...].T


def last_kernel(width, off_ref, amps_ref, kept_ref, sum_ref, out_ref, acc_ref):
    acc_ref[...] = jnp.zeros_like(acc_ref)
    have = amps_ref.shape[1] // LANES
    for base in range(0, width, BLOCK):
        size = min(BLOCK, width - base)
        count = -(-size // LANES)
        parts = shifted(off_ref, amps_ref, base, count, have - base // LANES)
        whole = size // LANES
        if whole:
            amps = jnp.concatenate([p.astype(jnp.bfloat16) for p in parts[:whole]], axis=1)
            acc_ref[...] += dot(kept_ref[:, pl.ds(base, whole * LANES)], amps)
        if whole < count:
            valid = size - whole * LANES
            amps = parts[whole].astype(jnp.bfloat16)[:, :valid]
            acc_ref[...] += dot(kept_ref[:, pl.ds(base + whole * LANES, valid)], amps)
    out_ref[...] = acc_ref[...].T + sum_ref[...]


def products(shift, amps, flat, cut, late, kept):
    pairs = amps.shape[0]
    rows, slab = flat.shape
    vmem = pl.BlockSpec(memory_space=pltpu.VMEM)
    smem = pl.BlockSpec(memory_space=pltpu.SMEM)
    total = jax.ShapeDtypeStruct((pairs, rows), jnp.float32)
    acc = [pltpu.VMEM((rows, pairs), jnp.float32)]
    first = pl.pallas_call(
        functools.partial(first_kernel, cut // BLOCK),
        out_shape=total,
        in_specs=[smem, vmem, pl.BlockSpec(memory_space=pl.ANY)],
        out_specs=vmem,
        scratch_shapes=acc,
        compiler_params=pltpu.CompilerParams(vmem_limit_bytes=LIMIT),
        cost_estimate=pl.CostEstimate(
            flops=2 * pairs * rows * cut, bytes_accessed=2 * rows * cut, transcendentals=0
        ),
        name="first_product",
    )(shift, amps, flat)
    return pl.pallas_call(
        functools.partial(last_kernel, slab - cut),
        out_shape=total,
        in_specs=[smem, vmem, vmem, vmem],
        out_specs=vmem,
        scratch_shapes=acc,
        compiler_params=pltpu.CompilerParams(vmem_limit_bytes=LIMIT),
        cost_estimate=pl.CostEstimate(
            flops=2 * pairs * rows * (slab - cut), bytes_accessed=2 * rows * (slab - cut), transcendentals=0
        ),
        name="last_product",
    )(shift, late, kept, first)


def exchange_sum(blocks, names):
    count = blocks.shape[0]
    me = lax.axis_index(names)
    terms = [lax.dynamic_index_in_dim(blocks, me, 0, keepdims=False)]
    power = count & (count - 1) == 0
    for step in range(count - 1, 0, -1):
        to = (lambda i: i ^ step) if power else (lambda i: (i + step) % count)
        block = lax.dynamic_index_in_dim(blocks, to(me), 0, keepdims=False)
        terms.append(lax.ppermute(block, names, [(i, to(i)) for i in range(count)]))
    return sum(terms[1:], terms[0])


def shards(amplitudes, integrals):
    z, x, core, col = (lax.axis_size(name) for name in ALL)
    count = z * x * core * col
    pair_local, full_width = amplitudes.shape
    slab = full_width // count
    window, virtuals, _ = integrals.shape
    rows = window * virtuals
    flat = integrals.reshape(rows, slab)

    begins = [d * slab // LANES * LANES for d in range(count)]
    most = max(1, max(d * slab - begins[d] for d in range(count)))
    off = lax.rem(lax.axis_index(ALL) * slab, LANES)
    shift = jnp.stack([off, lax.rem(LANES - off, LANES)]).astype(jnp.int32)

    blocks = -(-slab // BLOCK)
    cut = max(1, min(blocks - 1, round(FIRST * blocks))) * BLOCK
    sent, widths = [], []
    for low, high in ((0, cut), (cut, slab)):
        widths.append(-(-(most + high - low) // LANES) * LANES)
        sent.append(windows(amplitudes, [b + low for b in begins], widths[-1]))
    here = lax.all_to_all(sent[0], ALL, split_axis=0, concat_axis=0, tiled=True)
    kept = lax.slice(flat, (0, cut), (rows, slab))
    later, here, kept = lax.optimization_barrier((sent[1], here, kept))
    late = lax.all_to_all(later, ALL, split_axis=0, concat_axis=0, tiled=True)
    pairs = count * pair_local
    here, late = here.reshape(pairs, widths[0]), late.reshape(pairs, widths[1])
    total = products(shift, here, flat, cut, late, kept)

    part = total.reshape(z, x, core, col, pair_local, rows)
    part = exchange_sum(part.transpose(2, 0, 1, 3, 4, 5).reshape(core, z, x * col, pair_local, rows), "core")
    part = exchange_sum(part.transpose(1, 0, 2, 3), ("x", "col"))
    part = exchange_sum(part, "z")
    return part.reshape(pair_local, window, virtuals)


def solution(mesh):
    devices = mesh.devices
    row, col = devices.shape
    split = Mesh(devices.reshape(row // 4, 2, 2, col), ALL)
    return jax.shard_map(
        shards,
        mesh=split,
        in_specs=(P(ALL, None), P(None, None, ALL)),
        out_specs=P(ALL, None, None),
        check_vma=False,
    )
```

```python
import functools

import jax
import jax.numpy as jnp
from jax import lax
from jax.experimental import pallas as pl
from jax.experimental.pallas import tpu as pltpu
from jax.sharding import Mesh, PartitionSpec as P

ALL = ("z", "x", "core", "col")
LANES = 128
BLOCK = 1280
BUFFERS = 3
AHEAD = 2
LIMIT = 20 * 1024 * 1024
FIRST = 0.7


def window_kernel(starts, x_ref, o_ref):
    width = o_ref.shape[2]
    for index, start in enumerate(starts):
        size = min(width, x_ref.shape[1] - start)
        o_ref[index, :, pl.ds(0, size)] = x_ref[:, pl.ds(start, size)]


def windows(x, starts, width):
    return pl.pallas_call(
        functools.partial(window_kernel, starts),
        out_shape=jax.ShapeDtypeStruct((len(starts), x.shape[0], width), x.dtype),
        in_specs=[pl.BlockSpec(memory_space=pltpu.VMEM)],
        out_specs=pl.BlockSpec(memory_space=pltpu.VMEM),
        compiler_params=pltpu.CompilerParams(vmem_limit_bytes=16 * 1024 * 1024),
        cost_estimate=pl.CostEstimate(
            flops=0, bytes_accessed=4 * len(starts) * x.shape[0] * width, transcendentals=0
        ),
        name="windows",
    )(x)


def dot(ints, amps):
    return lax.dot_general(ints, amps, (((1,), (1,)), ((), ())), preferred_element_type=jnp.float32)


def shifted(off_ref, amps_ref, base, count, limit):
    lane = lax.broadcasted_iota(jnp.int32, (amps_ref.shape[0], LANES), 1)
    from_here = lane < LANES - off_ref[0]
    rolled = []
    for t in range(min(count + 1, limit)):
        tile = amps_ref[:, pl.ds(pl.multiple_of(base + t * LANES, LANES), LANES)]
        rolled.append(pltpu.roll(tile.astype(jnp.float32), off_ref[1], 1))
    return [
        jnp.where(from_here, rolled[t], rolled[min(t + 1, len(rolled) - 1)]) for t in range(count)
    ]


def first_kernel(steps, off_ref, amps_ref, ints_hbm, out_ref, acc_ref):
    acc_ref[...] = jnp.zeros_like(acc_ref)

    def body(ints_ref):
        step = pl.program_id(0)
        parts = shifted(off_ref, amps_ref, step * BLOCK, BLOCK // LANES, BLOCK // LANES + 1)
        amps = jnp.concatenate([p.astype(jnp.bfloat16) for p in parts], axis=1)
        acc_ref[...] += dot(ints_ref[...], amps)

    spec = pl.BlockSpec(
        (ints_hbm.shape[0], BLOCK), lambda j: (0, j), pipeline_mode=pl.Buffered(BUFFERS)
    )
    pltpu.emit_pipeline(body, grid=(steps,), in_specs=[spec])(ints_hbm)
    out_ref[...] = acc_ref[...].T


def last_kernel(pieces, off_ref, amps_ref, ints_hbm, sum_ref, out_ref, acc_ref, sems, *buffers):
    low = pieces[0][0]
    copies = [
        pltpu.make_async_copy(
            ints_hbm.at[:, pl.ds(start, size)], buffers[i], sems.at[i]
        )
        for i, (start, size) in enumerate(pieces)
    ]
    for copy in copies[:AHEAD]:
        copy.start()
    acc_ref[...] = jnp.zeros_like(acc_ref)
    have = amps_ref.shape[1] // LANES
    for i, (start, size) in enumerate(pieces):
        base = start - low
        count = -(-size // LANES)
        parts = shifted(off_ref, amps_ref, base, count, have - base // LANES)
        amps = jnp.concatenate([p.astype(jnp.bfloat16) for p in parts], axis=1)[:, :size]
        copies[i].wait()
        if i + AHEAD < len(copies):
            copies[i + AHEAD].start()
        acc_ref[...] += dot(buffers[i][...], amps)
    out_ref[...] = acc_ref[...].T + sum_ref[...]


def products(shift, amps, flat, cut, late):
    pairs = amps.shape[0]
    rows, slab = flat.shape
    vmem = pl.BlockSpec(memory_space=pltpu.VMEM)
    smem = pl.BlockSpec(memory_space=pltpu.SMEM)
    total = jax.ShapeDtypeStruct((pairs, rows), jnp.float32)
    acc = [pltpu.VMEM((rows, pairs), jnp.float32)]
    first = pl.pallas_call(
        functools.partial(first_kernel, cut // BLOCK),
        out_shape=total,
        in_specs=[smem, vmem, pl.BlockSpec(memory_space=pl.ANY)],
        out_specs=vmem,
        scratch_shapes=acc,
        compiler_params=pltpu.CompilerParams(vmem_limit_bytes=LIMIT),
        cost_estimate=pl.CostEstimate(
            flops=2 * pairs * rows * cut, bytes_accessed=2 * rows * cut, transcendentals=0
        ),
        name="first_product",
    )(shift, amps, flat)
    pieces = [(cut, min(BLOCK // 2, slab - cut))]
    while sum(pieces[-1]) < slab:
        start = sum(pieces[-1])
        pieces.append((start, min(BLOCK, slab - start)))
    return pl.pallas_call(
        functools.partial(last_kernel, pieces),
        out_shape=total,
        in_specs=[smem, vmem, pl.BlockSpec(memory_space=pl.ANY), vmem],
        out_specs=vmem,
        scratch_shapes=acc
        + [pltpu.SemaphoreType.DMA((len(pieces),))]
        + [pltpu.VMEM((rows, size), flat.dtype) for _, size in pieces],
        compiler_params=pltpu.CompilerParams(vmem_limit_bytes=36 * 1024 * 1024),
        cost_estimate=pl.CostEstimate(
            flops=2 * pairs * rows * (slab - cut),
            bytes_accessed=2 * rows * (slab - cut),
            transcendentals=0,
        ),
        name="last_product",
    )(shift, late, flat, first)


def exchange_sum(blocks, names):
    count = blocks.shape[0]
    me = lax.axis_index(names)
    terms = [lax.dynamic_index_in_dim(blocks, me, 0, keepdims=False)]
    power = count & (count - 1) == 0
    for step in range(count - 1, 0, -1):
        to = (lambda i: i ^ step) if power else (lambda i: (i + step) % count)
        block = lax.dynamic_index_in_dim(blocks, to(me), 0, keepdims=False)
        terms.append(lax.ppermute(block, names, [(i, to(i)) for i in range(count)]))
    return sum(terms[1:], terms[0])


def shards(amplitudes, integrals):
    z, x, core, col = (lax.axis_size(name) for name in ALL)
    count = z * x * core * col
    pair_local, full_width = amplitudes.shape
    slab = full_width // count
    window, virtuals, _ = integrals.shape
    rows = window * virtuals
    flat = integrals.reshape(rows, slab)

    begins = [d * slab // LANES * LANES for d in range(count)]
    most = max(1, max(d * slab - begins[d] for d in range(count)))
    off = lax.rem(lax.axis_index(ALL) * slab, LANES)
    shift = jnp.stack([off, lax.rem(LANES - off, LANES)]).astype(jnp.int32)

    blocks = -(-slab // BLOCK)
    cut = max(1, min(blocks - 1, round(FIRST * blocks))) * BLOCK
    sent, widths = [], []
    for low, high in ((0, cut), (cut, slab)):
        widths.append(-(-(most + high - low) // LANES) * LANES)
        sent.append(windows(amplitudes, [b + low for b in begins], widths[-1]))
    here = lax.all_to_all(sent[0], ALL, split_axis=0, concat_axis=0, tiled=True)
    later, here = lax.optimization_barrier((sent[1], here))
    late = lax.all_to_all(later, ALL, split_axis=0, concat_axis=0, tiled=True)
    pairs = count * pair_local
    here, late = here.reshape(pairs, widths[0]), late.reshape(pairs, widths[1])
    total = products(shift, here, flat, cut, late)

    part = total.reshape(z, x, core, col, pair_local, rows)
    part = exchange_sum(part.transpose(2, 0, 1, 3, 4, 5).reshape(core, z, x * col, pair_local, rows), "core")
    part = part.transpose(1, 0, 2, 3)
    part = lax.all_to_all(part, ("x", "col"), split_axis=0, concat_axis=0, tiled=True).sum(axis=0)
    part = lax.all_to_all(part, "z", split_axis=0, concat_axis=0, tiled=True).sum(axis=0)
    return part.reshape(pair_local, window, virtuals)


def solution(mesh):
    devices = mesh.devices
    row, col = devices.shape
    split = Mesh(devices.reshape(row // 4, 2, 2, col), ALL)
    return jax.shard_map(
        shards,
        mesh=split,
        in_specs=(P(ALL, None), P(None, None, ALL)),
        out_specs=P(ALL, None, None),
        check_vma=False,
    )
```

```python
import functools

import jax
import jax.numpy as jnp
from jax import lax
from jax.experimental import pallas as pl
from jax.experimental.pallas import tpu as pltpu
from jax.sharding import PartitionSpec as P

ALL = ("row", "col")
LANES = 128
BLOCK = 1280
BUFFERS = 3
PIECE = 768
LIMIT = 20 * 1024 * 1024
FIRST = 0.7


def window_kernel(starts, x_ref, o_ref):
    width = o_ref.shape[2]
    for index, start in enumerate(starts):
        size = min(width, x_ref.shape[1] - start)
        o_ref[index, :, pl.ds(0, size)] = x_ref[:, pl.ds(start, size)]


def windows(x, starts, width):
    return pl.pallas_call(
        functools.partial(window_kernel, starts),
        out_shape=jax.ShapeDtypeStruct((len(starts), x.shape[0], width), x.dtype),
        in_specs=[pl.BlockSpec(memory_space=pltpu.VMEM)],
        out_specs=pl.BlockSpec(memory_space=pltpu.VMEM),
        compiler_params=pltpu.CompilerParams(vmem_limit_bytes=16 * 1024 * 1024),
        cost_estimate=pl.CostEstimate(
            flops=0, bytes_accessed=4 * len(starts) * x.shape[0] * width, transcendentals=0
        ),
        name="windows",
    )(x)


def dot(ints, amps):
    return lax.dot_general(ints, amps, (((1,), (1,)), ((), ())), preferred_element_type=jnp.float32)


def shifted(off_ref, amps_ref, base, count, limit):
    lane = lax.broadcasted_iota(jnp.int32, (amps_ref.shape[0], LANES), 1)
    from_here = lane < LANES - off_ref[0]
    rolled = []
    for t in range(min(count + 1, limit)):
        tile = amps_ref[:, pl.ds(pl.multiple_of(base + t * LANES, LANES), LANES)]
        rolled.append(pltpu.roll(tile.astype(jnp.float32), off_ref[1], 1))
    return [
        jnp.where(from_here, rolled[t], rolled[min(t + 1, len(rolled) - 1)]) for t in range(count)
    ]


def first_kernel(steps, off_ref, amps_ref, ints_hbm, out_ref, acc_ref):
    acc_ref[...] = jnp.zeros_like(acc_ref)

    def body(ints_ref):
        step = pl.program_id(0)
        parts = shifted(off_ref, amps_ref, step * BLOCK, BLOCK // LANES, BLOCK // LANES + 1)
        amps = jnp.concatenate([p.astype(jnp.bfloat16) for p in parts], axis=1)
        acc_ref[...] += dot(ints_ref[...], amps)

    spec = pl.BlockSpec(
        (ints_hbm.shape[0], BLOCK), lambda j: (0, j), pipeline_mode=pl.Buffered(BUFFERS)
    )
    pltpu.emit_pipeline(body, grid=(steps,), in_specs=[spec])(ints_hbm)
    out_ref[...] = acc_ref[...].T


def last_kernel(pieces, off_ref, amps_ref, ints_hbm, sum_ref, out_ref, acc_ref, sems, *buffers):
    low = pieces[0][0]
    copies = [
        pltpu.make_async_copy(
            ints_hbm.at[:, pl.ds(start, size)], buffers[i], sems.at[i]
        )
        for i, (start, size) in enumerate(pieces)
    ]
    for copy in copies:
        copy.start()
    acc_ref[...] = jnp.zeros_like(acc_ref)
    have = amps_ref.shape[1] // LANES
    for i, (start, size) in enumerate(pieces):
        base = start - low
        count = -(-size // LANES)
        parts = shifted(off_ref, amps_ref, base, count, have - base // LANES)
        amps = jnp.concatenate([p.astype(jnp.bfloat16) for p in parts], axis=1)[:, :size]
        copies[i].wait()
        acc_ref[...] += dot(buffers[i][...], amps)
    out_ref[...] = acc_ref[...].T + sum_ref[...]


def products(shift, amps, flat, cut, late):
    pairs = amps.shape[0]
    rows, slab = flat.shape
    vmem = pl.BlockSpec(memory_space=pltpu.VMEM)
    smem = pl.BlockSpec(memory_space=pltpu.SMEM)
    total = jax.ShapeDtypeStruct((pairs, rows), jnp.float32)
    acc = [pltpu.VMEM((rows, pairs), jnp.float32)]
    first = pl.pallas_call(
        functools.partial(first_kernel, cut // BLOCK),
        out_shape=total,
        in_specs=[smem, vmem, pl.BlockSpec(memory_space=pl.ANY)],
        out_specs=vmem,
        scratch_shapes=acc,
        compiler_params=pltpu.CompilerParams(vmem_limit_bytes=LIMIT),
        cost_estimate=pl.CostEstimate(
            flops=2 * pairs * rows * cut, bytes_accessed=2 * rows * cut, transcendentals=0
        ),
        name="first_product",
    )(shift, amps, flat)
    pieces = [(start, min(PIECE, slab - start)) for start in range(cut, slab, PIECE)]
    return pl.pallas_call(
        functools.partial(last_kernel, pieces),
        out_shape=total,
        in_specs=[smem, vmem, pl.BlockSpec(memory_space=pl.ANY), vmem],
        out_specs=vmem,
        scratch_shapes=acc
        + [pltpu.SemaphoreType.DMA((len(pieces),))]
        + [pltpu.VMEM((rows, size), flat.dtype) for _, size in pieces],
        compiler_params=pltpu.CompilerParams(vmem_limit_bytes=36 * 1024 * 1024),
        cost_estimate=pl.CostEstimate(
            flops=2 * pairs * rows * (slab - cut),
            bytes_accessed=2 * rows * (slab - cut),
            transcendentals=0,
        ),
        name="last_product",
    )(shift, late, flat, first)


def shards(amplitudes, integrals):
    count = lax.axis_size("row") * lax.axis_size("col")
    pair_local, full_width = amplitudes.shape
    slab = full_width // count
    window, virtuals, _ = integrals.shape
    rows = window * virtuals
    flat = integrals.reshape(rows, slab)

    begins = [d * slab // LANES * LANES for d in range(count)]
    most = max(1, max(d * slab - begins[d] for d in range(count)))
    off = lax.rem(lax.axis_index(ALL) * slab, LANES)
    shift = jnp.stack([off, lax.rem(LANES - off, LANES)]).astype(jnp.int32)

    blocks = -(-slab // BLOCK)
    cut = max(1, min(blocks - 1, round(FIRST * blocks))) * BLOCK
    sent, widths = [], []
    for low, high in ((0, cut), (cut, slab)):
        widths.append(-(-(most + high - low) // LANES) * LANES)
        sent.append(windows(amplitudes, [b + low for b in begins], widths[-1]))
    here = lax.all_to_all(sent[0], ALL, split_axis=0, concat_axis=0, tiled=True)
    later, here = lax.optimization_barrier((sent[1], here))
    late = lax.all_to_all(later, ALL, split_axis=0, concat_axis=0, tiled=True)
    pairs = count * pair_local
    here, late = here.reshape(pairs, widths[0]), late.reshape(pairs, widths[1])
    total = products(shift, here, flat, cut, late)

    part = total.reshape(count, pair_local, rows)
    part = lax.all_to_all(part, ALL, split_axis=0, concat_axis=0, tiled=True).sum(axis=0)
    return part.reshape(pair_local, window, virtuals)


def solution(mesh):
    return jax.shard_map(
        shards,
        mesh=mesh,
        in_specs=(P(ALL, None), P(None, None, ALL)),
        out_specs=P(ALL, None, None),
        check_vma=False,
    )
```

```python
import functools

import jax
import jax.numpy as jnp
from jax import lax
from jax.experimental import pallas as pl
from jax.experimental.pallas import tpu as pltpu
from jax.sharding import Mesh, PartitionSpec as P

ALL = ("z", "x", "core", "col")
LANES = 128
BLOCK = 1280
BUFFERS = 3
AHEAD = 2
LIMIT = 20 * 1024 * 1024
FIRST = 0.7


def window_kernel(starts, x_ref, o_ref):
    width = o_ref.shape[2]
    for index, start in enumerate(starts):
        size = min(width, x_ref.shape[1] - start)
        o_ref[index, :, pl.ds(0, size)] = x_ref[:, pl.ds(start, size)]


def windows(x, starts, width):
    return pl.pallas_call(
        functools.partial(window_kernel, starts),
        out_shape=jax.ShapeDtypeStruct((len(starts), x.shape[0], width), x.dtype),
        in_specs=[pl.BlockSpec(memory_space=pltpu.VMEM)],
        out_specs=pl.BlockSpec(memory_space=pltpu.VMEM),
        compiler_params=pltpu.CompilerParams(vmem_limit_bytes=16 * 1024 * 1024),
        cost_estimate=pl.CostEstimate(
            flops=0, bytes_accessed=4 * len(starts) * x.shape[0] * width, transcendentals=0
        ),
        name="windows",
    )(x)


def dot(amps, ints):
    return lax.dot_general(amps, ints, (((1,), (1,)), ((), ())), preferred_element_type=jnp.float32)


def shifted(off_ref, amps_ref, base, count, limit):
    lane = lax.broadcasted_iota(jnp.int32, (amps_ref.shape[0], LANES), 1)
    from_here = lane < LANES - off_ref[0]
    rolled = []
    for t in range(min(count + 1, limit)):
        tile = amps_ref[:, pl.ds(pl.multiple_of(base + t * LANES, LANES), LANES)]
        rolled.append(pltpu.roll(tile.astype(jnp.float32), off_ref[1], 1))
    return [
        jnp.where(from_here, rolled[t], rolled[min(t + 1, len(rolled) - 1)]) for t in range(count)
    ]


def first_kernel(steps, off_ref, amps_ref, ints_hbm, out_ref, acc_ref):
    acc_ref[...] = jnp.zeros_like(acc_ref)

    def body(ints_ref):
        step = pl.program_id(0)
        parts = shifted(off_ref, amps_ref, step * BLOCK, BLOCK // LANES, BLOCK // LANES + 1)
        amps = jnp.concatenate([p.astype(jnp.bfloat16) for p in parts], axis=1)
        acc_ref[...] += dot(amps, ints_ref[...])

    spec = pl.BlockSpec(
        (ints_hbm.shape[0], BLOCK), lambda j: (0, j), pipeline_mode=pl.Buffered(BUFFERS)
    )
    pltpu.emit_pipeline(body, grid=(steps,), in_specs=[spec])(ints_hbm)
    out_ref[...] = acc_ref[...]


def last_kernel(pieces, off_ref, amps_ref, ints_hbm, sum_ref, out_ref, acc_ref, sems, *buffers):
    low = pieces[0][0]
    copies = [
        pltpu.make_async_copy(
            ints_hbm.at[:, pl.ds(start, size)], buffers[i], sems.at[i]
        )
        for i, (start, size) in enumerate(pieces)
    ]
    for copy in copies[:AHEAD]:
        copy.start()
    acc_ref[...] = jnp.zeros_like(acc_ref)
    have = amps_ref.shape[1] // LANES
    for i, (start, size) in enumerate(pieces):
        base = start - low
        count = -(-size // LANES)
        parts = shifted(off_ref, amps_ref, base, count, have - base // LANES)
        amps = jnp.concatenate([p.astype(jnp.bfloat16) for p in parts], axis=1)[:, :size]
        copies[i].wait()
        if i + AHEAD < len(copies):
            copies[i + AHEAD].start()
        acc_ref[...] += dot(amps, buffers[i][...])
    out_ref[...] = acc_ref[...] + sum_ref[...]


def products(shift, amps, flat, cut, late):
    pairs = amps.shape[0]
    rows, slab = flat.shape
    vmem = pl.BlockSpec(memory_space=pltpu.VMEM)
    smem = pl.BlockSpec(memory_space=pltpu.SMEM)
    total = jax.ShapeDtypeStruct((pairs, rows), jnp.float32)
    acc = [pltpu.VMEM((pairs, rows), jnp.float32)]
    first = pl.pallas_call(
        functools.partial(first_kernel, cut // BLOCK),
        out_shape=total,
        in_specs=[smem, vmem, pl.BlockSpec(memory_space=pl.ANY)],
        out_specs=vmem,
        scratch_shapes=acc,
        compiler_params=pltpu.CompilerParams(vmem_limit_bytes=LIMIT),
        cost_estimate=pl.CostEstimate(
            flops=2 * pairs * rows * cut, bytes_accessed=2 * rows * cut, transcendentals=0
        ),
        name="first_product",
    )(shift, amps, flat)
    pieces = [(cut, min(BLOCK // 2, slab - cut))]
    while sum(pieces[-1]) < slab:
        start = sum(pieces[-1])
        pieces.append((start, min(BLOCK, slab - start)))
    return pl.pallas_call(
        functools.partial(last_kernel, pieces),
        out_shape=total,
        in_specs=[smem, vmem, pl.BlockSpec(memory_space=pl.ANY), vmem],
        out_specs=vmem,
        scratch_shapes=acc
        + [pltpu.SemaphoreType.DMA((len(pieces),))]
        + [pltpu.VMEM((rows, size), flat.dtype) for _, size in pieces],
        compiler_params=pltpu.CompilerParams(vmem_limit_bytes=36 * 1024 * 1024),
        cost_estimate=pl.CostEstimate(
            flops=2 * pairs * rows * (slab - cut),
            bytes_accessed=2 * rows * (slab - cut),
            transcendentals=0,
        ),
        name="last_product",
    )(shift, late, flat, first)


def exchange_sum(blocks, names):
    count = blocks.shape[0]
    me = lax.axis_index(names)
    terms = [lax.dynamic_index_in_dim(blocks, me, 0, keepdims=False)]
    power = count & (count - 1) == 0
    for step in range(count - 1, 0, -1):
        to = (lambda i: i ^ step) if power else (lambda i: (i + step) % count)
        block = lax.dynamic_index_in_dim(blocks, to(me), 0, keepdims=False)
        terms.append(lax.ppermute(block, names, [(i, to(i)) for i in range(count)]))
    return sum(terms[1:], terms[0])


def shards(amplitudes, integrals):
    z, x, core, col = (lax.axis_size(name) for name in ALL)
    count = z * x * core * col
    pair_local, full_width = amplitudes.shape
    slab = full_width // count
    window, virtuals, _ = integrals.shape
    rows = window * virtuals
    flat = integrals.reshape(rows, slab)

    begins = [d * slab // LANES * LANES for d in range(count)]
    most = max(1, max(d * slab - begins[d] for d in range(count)))
    off = lax.rem(lax.axis_index(ALL) * slab, LANES)
    shift = jnp.stack([off, lax.rem(LANES - off, LANES)]).astype(jnp.int32)

    blocks = -(-slab // BLOCK)
    cut = max(1, min(blocks - 1, round(FIRST * blocks))) * BLOCK
    sent, widths = [], []
    for low, high in ((0, cut), (cut, slab)):
        widths.append(-(-(most + high - low) // LANES) * LANES)
        sent.append(windows(amplitudes, [b + low for b in begins], widths[-1]))
    here = lax.all_to_all(sent[0], ALL, split_axis=0, concat_axis=0, tiled=True)
    later, here = lax.optimization_barrier((sent[1], here))
    late = lax.all_to_all(later, ALL, split_axis=0, concat_axis=0, tiled=True)
    pairs = count * pair_local
    here, late = here.reshape(pairs, widths[0]), late.reshape(pairs, widths[1])
    total = products(shift, here, flat, cut, late)

    part = total.reshape(z, x, core, col, pair_local, rows)
    part = exchange_sum(part.transpose(2, 0, 1, 3, 4, 5).reshape(core, z, x * col, pair_local, rows), "core")
    part = exchange_sum(part.transpose(1, 0, 2, 3), ("x", "col"))
    part = exchange_sum(part, "z")
    return part.reshape(pair_local, window, virtuals)


def solution(mesh):
    devices = mesh.devices
    row, col = devices.shape
    split = Mesh(devices.reshape(row // 4, 2, 2, col), ALL)
    return jax.shard_map(
        shards,
        mesh=split,
        in_specs=(P(ALL, None), P(None, None, ALL)),
        out_specs=P(ALL, None, None),
        check_vma=False,
    )
```

```python
import functools

import jax
import jax.numpy as jnp
from jax import lax
from jax.experimental import pallas as pl
from jax.experimental.pallas import tpu as pltpu
from jax.sharding import Mesh, PartitionSpec as P

ALL = ("z", "x", "core", "col")
LANES = 128
BLOCK = 1280
BUFFERS = 3
AHEAD = 2
LIMIT = 20 * 1024 * 1024
FIRST = 0.7


def window_kernel(starts, x_ref, o_ref):
    width = o_ref.shape[2]
    for index, start in enumerate(starts):
        size = min(width, x_ref.shape[1] - start)
        o_ref[index, :, pl.ds(0, size)] = x_ref[:, pl.ds(start, size)]


def windows(x, starts, width):
    return pl.pallas_call(
        functools.partial(window_kernel, starts),
        out_shape=jax.ShapeDtypeStruct((len(starts), x.shape[0], width), x.dtype),
        in_specs=[pl.BlockSpec(memory_space=pltpu.VMEM)],
        out_specs=pl.BlockSpec(memory_space=pltpu.VMEM),
        compiler_params=pltpu.CompilerParams(vmem_limit_bytes=16 * 1024 * 1024),
        cost_estimate=pl.CostEstimate(
            flops=0, bytes_accessed=4 * len(starts) * x.shape[0] * width, transcendentals=0
        ),
        name="windows",
    )(x)


def dot(left, right):
    return lax.dot_general(left, right, (((1,), (1,)), ((), ())), preferred_element_type=jnp.float32)


def shifted(off_ref, amps_ref, base, count, limit):
    lane = lax.broadcasted_iota(jnp.int32, (amps_ref.shape[0], LANES), 1)
    from_here = lane < LANES - off_ref[0]
    rolled = []
    for t in range(min(count + 1, limit)):
        tile = amps_ref[:, pl.ds(pl.multiple_of(base + t * LANES, LANES), LANES)]
        rolled.append(pltpu.roll(tile.astype(jnp.float32), off_ref[1], 1))
    return [
        jnp.where(from_here, rolled[t], rolled[min(t + 1, len(rolled) - 1)]) for t in range(count)
    ]


def first_kernel(steps, off_ref, amps_ref, ints_hbm, out_ref, acc_ref):
    acc_ref[...] = jnp.zeros_like(acc_ref)

    def body(ints_ref):
        step = pl.program_id(0)
        parts = shifted(off_ref, amps_ref, step * BLOCK, BLOCK // LANES, BLOCK // LANES + 1)
        amps = jnp.concatenate([p.astype(jnp.bfloat16) for p in parts], axis=1)
        acc_ref[...] += dot(ints_ref[...], amps)

    spec = pl.BlockSpec(
        (ints_hbm.shape[0], BLOCK), lambda j: (0, j), pipeline_mode=pl.Buffered(BUFFERS)
    )
    pltpu.emit_pipeline(body, grid=(steps,), in_specs=[spec])(ints_hbm)
    out_ref[...] = acc_ref[...].T


def last_kernel(pieces, off_ref, amps_ref, ints_hbm, sum_ref, out_ref, acc_ref, sems, *buffers):
    low = pieces[0][0]
    copies = [
        pltpu.make_async_copy(
            ints_hbm.at[:, pl.ds(start, size)], buffers[i], sems.at[i]
        )
        for i, (start, size) in enumerate(pieces)
    ]
    for copy in copies[:AHEAD]:
        copy.start()
    acc_ref[...] = jnp.zeros_like(acc_ref)
    have = amps_ref.shape[1] // LANES
    for i, (start, size) in enumerate(pieces):
        base = start - low
        count = -(-size // LANES)
        parts = shifted(off_ref, amps_ref, base, count, have - base // LANES)
        amps = jnp.concatenate([p.astype(jnp.bfloat16) for p in parts], axis=1)[:, :size]
        copies[i].wait()
        if i + AHEAD < len(copies):
            copies[i + AHEAD].start()
        acc_ref[...] += dot(amps, buffers[i][...])
    out_ref[...] = acc_ref[...] + sum_ref[...]


def products(shift, amps, flat, cut, late):
    pairs = amps.shape[0]
    rows, slab = flat.shape
    vmem = pl.BlockSpec(memory_space=pltpu.VMEM)
    smem = pl.BlockSpec(memory_space=pltpu.SMEM)
    total = jax.ShapeDtypeStruct((pairs, rows), jnp.float32)
    first = pl.pallas_call(
        functools.partial(first_kernel, cut // BLOCK),
        out_shape=total,
        in_specs=[smem, vmem, pl.BlockSpec(memory_space=pl.ANY)],
        out_specs=vmem,
        scratch_shapes=[pltpu.VMEM((rows, pairs), jnp.float32)],
        compiler_params=pltpu.CompilerParams(vmem_limit_bytes=LIMIT),
        cost_estimate=pl.CostEstimate(
            flops=2 * pairs * rows * cut, bytes_accessed=2 * rows * cut, transcendentals=0
        ),
        name="first_product",
    )(shift, amps, flat)
    pieces = []
    start = cut
    while start < slab:
        size = min((384, 768)[len(pieces)] if len(pieces) < 2 else BLOCK, slab - start)
        pieces.append((start, size))
        start += size
    return pl.pallas_call(
        functools.partial(last_kernel, pieces),
        out_shape=total,
        in_specs=[smem, vmem, pl.BlockSpec(memory_space=pl.ANY), vmem],
        out_specs=vmem,
        scratch_shapes=[pltpu.VMEM((pairs, rows), jnp.float32)]
        + [pltpu.SemaphoreType.DMA((len(pieces),))]
        + [pltpu.VMEM((rows, size), flat.dtype) for _, size in pieces],
        compiler_params=pltpu.CompilerParams(vmem_limit_bytes=36 * 1024 * 1024),
        cost_estimate=pl.CostEstimate(
            flops=2 * pairs * rows * (slab - cut),
            bytes_accessed=2 * rows * (slab - cut),
            transcendentals=0,
        ),
        name="last_product",
    )(shift, late, flat, first)


def exchange_sum(blocks, names):
    count = blocks.shape[0]
    me = lax.axis_index(names)
    terms = [lax.dynamic_index_in_dim(blocks, me, 0, keepdims=False)]
    power = count & (count - 1) == 0
    for step in range(count - 1, 0, -1):
        to = (lambda i: i ^ step) if power else (lambda i: (i + step) % count)
        block = lax.dynamic_index_in_dim(blocks, to(me), 0, keepdims=False)
        terms.append(lax.ppermute(block, names, [(i, to(i)) for i in range(count)]))
    return sum(terms[1:], terms[0])


def shards(amplitudes, integrals):
    z, x, core, col = (lax.axis_size(name) for name in ALL)
    count = z * x * core * col
    pair_local, full_width = amplitudes.shape
    slab = full_width // count
    window, virtuals, _ = integrals.shape
    rows = window * virtuals
    flat = integrals.reshape(rows, slab)

    begins = [d * slab // LANES * LANES for d in range(count)]
    most = max(1, max(d * slab - begins[d] for d in range(count)))
    off = lax.rem(lax.axis_index(ALL) * slab, LANES)
    shift = jnp.stack([off, lax.rem(LANES - off, LANES)]).astype(jnp.int32)

    blocks = -(-slab // BLOCK)
    cut = max(1, min(blocks - 1, round(FIRST * blocks))) * BLOCK
    sent, widths = [], []
    for low, high in ((0, cut), (cut, slab)):
        widths.append(-(-(most + high - low) // LANES) * LANES)
        sent.append(windows(amplitudes, [b + low for b in begins], widths[-1]))
    here = lax.all_to_all(sent[0], ALL, split_axis=0, concat_axis=0, tiled=True)
    later, here = lax.optimization_barrier((sent[1], here))
    late = lax.all_to_all(later, ALL, split_axis=0, concat_axis=0, tiled=True)
    pairs = count * pair_local
    here, late = here.reshape(pairs, widths[0]), late.reshape(pairs, widths[1])
    total = products(shift, here, flat, cut, late)

    part = total.reshape(z, x, core, col, pair_local, rows)
    part = exchange_sum(part.transpose(2, 0, 1, 3, 4, 5).reshape(core, z, x * col, pair_local, rows), "core")
    part = exchange_sum(part.transpose(1, 0, 2, 3), ("x", "col"))
    part = exchange_sum(part, "z")
    return part.reshape(pair_local, window, virtuals)


def solution(mesh):
    devices = mesh.devices
    row, col = devices.shape
    split = Mesh(devices.reshape(row // 4, 2, 2, col), ALL)
    return jax.shard_map(
        shards,
        mesh=split,
        in_specs=(P(ALL, None), P(None, None, ALL)),
        out_specs=P(ALL, None, None),
        check_vma=False,
    )
```

```python
import functools

import jax
import jax.numpy as jnp
from jax import lax
from jax.experimental import pallas as pl
from jax.experimental.pallas import tpu as pltpu
from jax.sharding import Mesh, PartitionSpec as P

ALL = ("z", "x", "core", "col")
LANES = 128
BLOCK = 1280
BUFFERS = 3
AHEAD = 3
LIMIT = 20 * 1024 * 1024
FIRST = 0.7


def window_kernel(starts, x_ref, o_ref):
    width = o_ref.shape[2]
    for index, start in enumerate(starts):
        size = min(width, x_ref.shape[1] - start)
        o_ref[index, :, pl.ds(0, size)] = x_ref[:, pl.ds(start, size)]


def windows(x, starts, width):
    return pl.pallas_call(
        functools.partial(window_kernel, starts),
        out_shape=jax.ShapeDtypeStruct((len(starts), x.shape[0], width), x.dtype),
        in_specs=[pl.BlockSpec(memory_space=pltpu.VMEM)],
        out_specs=pl.BlockSpec(memory_space=pltpu.VMEM),
        compiler_params=pltpu.CompilerParams(vmem_limit_bytes=16 * 1024 * 1024),
        cost_estimate=pl.CostEstimate(
            flops=0, bytes_accessed=4 * len(starts) * x.shape[0] * width, transcendentals=0
        ),
        name="windows",
    )(x)


def dot(left, right):
    return lax.dot_general(left, right, (((1,), (1,)), ((), ())), preferred_element_type=jnp.float32)


def shifted(off_ref, amps_ref, base, count, limit):
    lane = lax.broadcasted_iota(jnp.int32, (amps_ref.shape[0], LANES), 1)
    from_here = lane < LANES - off_ref[0]
    rolled = []
    for t in range(min(count + 1, limit)):
        tile = amps_ref[:, pl.ds(pl.multiple_of(base + t * LANES, LANES), LANES)]
        rolled.append(pltpu.roll(tile.astype(jnp.float32), off_ref[1], 1))
    return [
        jnp.where(from_here, rolled[t], rolled[min(t + 1, len(rolled) - 1)]) for t in range(count)
    ]


def first_kernel(steps, off_ref, amps_ref, ints_hbm, out_ref, acc_ref):
    acc_ref[...] = jnp.zeros_like(acc_ref)

    def body(ints_ref):
        step = pl.program_id(0)
        parts = shifted(off_ref, amps_ref, step * BLOCK, BLOCK // LANES, BLOCK // LANES + 1)
        amps = jnp.concatenate([p.astype(jnp.bfloat16) for p in parts], axis=1)
        acc_ref[...] += dot(ints_ref[...], amps)

    spec = pl.BlockSpec(
        (ints_hbm.shape[0], BLOCK), lambda j: (0, j), pipeline_mode=pl.Buffered(BUFFERS)
    )
    pltpu.emit_pipeline(body, grid=(steps,), in_specs=[spec])(ints_hbm)
    out_ref[...] = acc_ref[...].T


def last_kernel(pieces, off_ref, amps_ref, ints_hbm, sum_ref, out_ref, acc_ref, sems, *buffers):
    low = pieces[0][0]
    copies = [
        pltpu.make_async_copy(
            ints_hbm.at[:, pl.ds(start, size)], buffers[i], sems.at[i]
        )
        for i, (start, size) in enumerate(pieces)
    ]
    for copy in copies[:AHEAD]:
        copy.start()
    acc_ref[...] = jnp.zeros_like(acc_ref)
    have = amps_ref.shape[1] // LANES
    for i, (start, size) in enumerate(pieces):
        base = start - low
        count = -(-size // LANES)
        parts = shifted(off_ref, amps_ref, base, count, have - base // LANES)
        amps = jnp.concatenate([p.astype(jnp.bfloat16) for p in parts], axis=1)[:, :size]
        copies[i].wait()
        if i + AHEAD < len(copies):
            copies[i + AHEAD].start()
        acc_ref[...] += dot(amps, buffers[i][...])
    out_ref[...] = acc_ref[...] + sum_ref[...]


def products(shift, amps, flat, cut, late):
    pairs = amps.shape[0]
    rows, slab = flat.shape
    vmem = pl.BlockSpec(memory_space=pltpu.VMEM)
    smem = pl.BlockSpec(memory_space=pltpu.SMEM)
    total = jax.ShapeDtypeStruct((pairs, rows), jnp.float32)
    first = pl.pallas_call(
        functools.partial(first_kernel, cut // BLOCK),
        out_shape=total,
        in_specs=[smem, vmem, pl.BlockSpec(memory_space=pl.ANY)],
        out_specs=vmem,
        scratch_shapes=[pltpu.VMEM((rows, pairs), jnp.float32)],
        compiler_params=pltpu.CompilerParams(vmem_limit_bytes=LIMIT),
        cost_estimate=pl.CostEstimate(
            flops=2 * pairs * rows * cut, bytes_accessed=2 * rows * cut, transcendentals=0
        ),
        name="first_product",
    )(shift, amps, flat)
    pieces = []
    start = cut
    while start < slab:
        size = min((384, 768)[len(pieces)] if len(pieces) < 2 else BLOCK, slab - start)
        pieces.append((start, size))
        start += size
    return pl.pallas_call(
        functools.partial(last_kernel, pieces),
        out_shape=total,
        in_specs=[smem, vmem, pl.BlockSpec(memory_space=pl.ANY), vmem],
        out_specs=vmem,
        scratch_shapes=[pltpu.VMEM((pairs, rows), jnp.float32)]
        + [pltpu.SemaphoreType.DMA((len(pieces),))]
        + [pltpu.VMEM((rows, size), flat.dtype) for _, size in pieces],
        compiler_params=pltpu.CompilerParams(vmem_limit_bytes=36 * 1024 * 1024),
        cost_estimate=pl.CostEstimate(
            flops=2 * pairs * rows * (slab - cut),
            bytes_accessed=2 * rows * (slab - cut),
            transcendentals=0,
        ),
        name="last_product",
    )(shift, late, flat, first)


def exchange_sum(blocks, names):
    count = blocks.shape[0]
    me = lax.axis_index(names)
    terms = [lax.dynamic_index_in_dim(blocks, me, 0, keepdims=False)]
    power = count & (count - 1) == 0
    for step in range(count - 1, 0, -1):
        to = (lambda i: i ^ step) if power else (lambda i: (i + step) % count)
        block = lax.dynamic_index_in_dim(blocks, to(me), 0, keepdims=False)
        terms.append(lax.ppermute(block, names, [(i, to(i)) for i in range(count)]))
    return sum(terms[1:], terms[0])


def shards(amplitudes, integrals):
    z, x, core, col = (lax.axis_size(name) for name in ALL)
    count = z * x * core * col
    pair_local, full_width = amplitudes.shape
    slab = full_width // count
    window, virtuals, _ = integrals.shape
    rows = window * virtuals
    flat = integrals.reshape(rows, slab)

    begins = [d * slab // LANES * LANES for d in range(count)]
    most = max(1, max(d * slab - begins[d] for d in range(count)))
    off = lax.rem(lax.axis_index(ALL) * slab, LANES)
    shift = jnp.stack([off, lax.rem(LANES - off, LANES)]).astype(jnp.int32)

    blocks = -(-slab // BLOCK)
    cut = max(1, min(blocks - 1, round(FIRST * blocks))) * BLOCK
    sent, widths = [], []
    for low, high in ((0, cut), (cut, slab)):
        widths.append(-(-(most + high - low) // LANES) * LANES)
        sent.append(windows(amplitudes, [b + low for b in begins], widths[-1]))
    here = lax.all_to_all(sent[0], ALL, split_axis=0, concat_axis=0, tiled=True)
    later, here = lax.optimization_barrier((sent[1], here))
    late = lax.all_to_all(later, ALL, split_axis=0, concat_axis=0, tiled=True)
    pairs = count * pair_local
    here, late = here.reshape(pairs, widths[0]), late.reshape(pairs, widths[1])
    total = products(shift, here, flat, cut, late)

    part = total.reshape(z, x, core, col, pair_local, rows)
    part = exchange_sum(part.transpose(2, 0, 1, 3, 4, 5).reshape(core, z, x * col, pair_local, rows), "core")
    part = exchange_sum(part.transpose(1, 0, 2, 3), ("x", "col"))
    part = exchange_sum(part, "z")
    return part.reshape(pair_local, window, virtuals)


def solution(mesh):
    devices = mesh.devices
    row, col = devices.shape
    split = Mesh(devices.reshape(row // 4, 2, 2, col), ALL)
    return jax.shard_map(
        shards,
        mesh=split,
        in_specs=(P(ALL, None), P(None, None, ALL)),
        out_specs=P(ALL, None, None),
        check_vma=False,
    )
```
